512 devices in a mesh: past: 8 (over y, core), second: 64 (over z, x).
Axes of the slice: x: 4, y: 4, z: 16, core: 2. Of those that a mesh axis runs over, the one named last changes fastest.
Arguments:
- green_row: float32 [1024, 64, 128], P('second'), may hold values from -4 to 4
- green_hist: float32 [32, 1024, 64, 128], P('past', 'second'), may hold values from -5.25 to 5.25, as said below
- hamiltonian: float32 [64, 128], replicated, may hold values from -0.75 to 0.75
- quad_table: float32 [8], replicated, may hold values from 0.2 to 2
- weight_index: int32 [32], P('past'), may hold values from 0 to 7
- block_start: int32 [1], replicated, may hold values from 0 to 992
Outputs:
- green_next: float32 [1024, 64, 128], P('second')
- change_norm: float32 [1], replicated
The draws below stay inside these ranges and needn't reach their ends.
Inputs may be any that keep to these rules, and one draw needn't show every extreme that they name: `green_hist`: real numbers of order one; magnitudes differ between second times.
All inputs are finite; a program needn't handle non-finite values.
Results may differ from the reference program's by a relative error of at most 0.0003.
Values sent between devices are 32-bit elements; how exact they have to be, the bound alone decides.
A program may use at most 64 MiB of HBM per device.

```python
import math
import jax
import jax.numpy as jnp
from jax import lax

NO = 64
SEC_DEV = 16
NQ = 8
PT = 32
NS = 1024
N_SECOND = 64


def draw_green_hist(key, part):
    scale_key = jax.random.fold_in(key, 11)
    value_key = jax.random.fold_in(key, 23)
    rough = jnp.exp(jax.random.uniform(scale_key, (NS,), jnp.float32, math.log(0.3), math.log(1.5)))
    rising = 3.0 ** (jnp.arange(NS, dtype=jnp.float32) / NS - 1.0)
    column_scale = (rough * rising)[None, :, None, None]
    values = jnp.clip(jax.random.normal(value_key, (PT, NS, NO, 2 * NO), jnp.float32), -3.5, 3.5)
    return (values * column_scale).astype(jnp.float32)


def set_ends(entries, key, smallest, top_value):
    extent = entries.shape
    place = [jax.random.randint(jax.random.fold_in(key, axis), (), 0, extent[axis]) for axis in range(len(extent))]
    entries = entries.at[tuple(place)].set(smallest)
    longest = extent.index(max(extent))
    place[longest] = (place[longest] + 1) % extent[longest]
    return entries.at[tuple(place)].set(top_value)


def block_scale(rng, dims, pieces, smallest, high):
    def one(dim, blocks):
        steps = jax.random.uniform(jax.random.fold_in(jax.random.fold_in(rng, 6), dim), (blocks,), jnp.float32, smallest / len(pieces), high / len(pieces))
        return jnp.repeat(jnp.exp(steps), dims[dim] // blocks).reshape((-1,) + (1,) * (len(dims) - dim - 1))

    loudness = one(*pieces[0])
    for cut in pieces[1:]:
        loudness = loudness * one(*cut)
    return loudness


def noise(own_key, extent, scale, most, pieces=(), kind=jnp.bfloat16):
    array = jax.random.normal(own_key, extent, jnp.float32) * scale
    if len(pieces) > 0:
        array = block_scale(own_key, extent, pieces, -0.22, 0.18) * array
    return jnp.clip(array, min=-most, max=most).astype(kind)


def setup_inputs(seed: int = 0) -> dict:
    streams_of = jax.random.split(jax.random.key(seed), 7)
    return {
        "green_row": noise(streams_of[0], (NS, NO, 2 * NO), 0.7, 4.0, ((0, 64),), jnp.float32),
        "green_hist": draw_green_hist(jax.random.fold_in(streams_of[6], 71), 0),
        "hamiltonian": noise(streams_of[2], (NO, 2 * NO), NO ** -0.5, 0.75, (), jnp.float32),
        "quad_table": jnp.clip(jnp.exp(jax.random.uniform(streams_of[3], (NQ,), jnp.float32, math.log(0.2), math.log(2.0))), 0.2, 2.0),
        "weight_index": set_ends(jax.random.randint(streams_of[4], (PT,), 0, NQ), jax.random.fold_in(streams_of[4], 1), 0, NQ - 1).astype(jnp.int32),
        "block_start": jax.random.randint(streams_of[5], (1,), 0, NS - PT + 1).astype(jnp.int32),
    }


coupling = 0.5
step_size = 0.25

def rotate(tiles):
    return jnp.concatenate([-tiles[..., NO:], tiles[..., :NO]], axis=-1)

def self_energy(tiles):
    magnitude = tiles[..., :NO] ** 2 + tiles[..., NO:] ** 2
    return -coupling * jnp.concatenate([magnitude, magnitude], axis=-1) * tiles

def apply_ham(herm_real, herm_imag, tiles):
    first = jnp.einsum('ij,sjk->sik', herm_real, tiles, precision=lax.Precision.HIGHEST)
    second = jnp.einsum('ij,sjk->sik', herm_imag, rotate(tiles), precision=lax.Precision.HIGHEST)
    return first + second

def memory(tiles_in, green_hist, weights, window_start):
    window = lax.dynamic_slice_in_dim(tiles_in, window_start, PT, 0)
    weight_col = weights[:, None, None]
    left_side = jnp.stack([weight_col * self_energy(window), weight_col * window])
    left_side = jnp.stack([left_side[..., :NO], left_side[..., NO:]])
    norm_scale = 1.0 / math.sqrt(NO * PT)

    def block(block_index):
        hist_block = lax.dynamic_slice_in_dim(green_hist, (block_index * SEC_DEV).astype(jnp.int32), SEC_DEV, 1)
        right_side = jnp.stack([hist_block, self_energy(hist_block)])
        contracted = jnp.einsum('cqpij,qpsjk->csik', left_side, right_side, precision=lax.Precision.HIGHEST)
        return norm_scale * (contracted[0] + rotate(contracted[1]))
    blocks = lax.map(block, jnp.arange(N_SECOND, dtype=jnp.int32))
    return blocks.reshape(NS, NO, 2 * NO)

def reference(green_row, green_hist, hamiltonian, quad_table, weight_index, block_start):
    ham_real = hamiltonian[:, :NO]
    ham_imag = hamiltonian[:, NO:]
    herm_real = 0.5 * (ham_real + ham_real.T)
    herm_imag = 0.5 * (ham_imag - ham_imag.T)
    weights = jnp.take(quad_table, weight_index, axis=0)
    window_start = block_start[0].astype(jnp.int32)

    def derive(tiles_in):
        combined = apply_ham(herm_real, herm_imag, tiles_in) + memory(tiles_in, green_hist, weights, window_start)
        return jnp.concatenate([combined[..., NO:], -combined[..., :NO]], axis=-1)
    slope_one = derive(green_row)
    predicted = green_row + step_size * slope_one
    slope_two = derive(predicted)
    green_next = green_row + 0.5 * step_size * (slope_one + slope_two)
    square_sum = jnp.sum((green_next - predicted) ** 2)
    change = jnp.sqrt(square_sum / (NS * NO * 2 * NO)) / step_size
    return (green_next, change.reshape(1))
```

```python
import functools
import math

import jax
import jax.numpy as jnp
from jax import lax
from jax.experimental import pallas as pl
from jax.experimental.pallas import tpu as pltpu
from jax.sharding import PartitionSpec as P

COUPLING = 0.5
STEP = 0.25
CHIPS_X = 4
LANES = 128
MESH = pl.DeviceIdType.MESH
F32 = jnp.float32
BF16 = jnp.bfloat16


def wait_bytes(ref, sem):
    pltpu.make_async_copy(ref, ref, sem).wait()


def send(src, dst, send_sem, recv_sem, where):
    pltpu.make_async_remote_copy(
        src_ref=src, dst_ref=dst, send_sem=send_sem, recv_sem=recv_sem, device_id=where, device_id_type=MESH
    ).start()


def split(values):
    high = values.astype(BF16).astype(F32)
    return high, values - high


def kernel(
    dims, start_ref, index_ref, table_ref, row_hbm, hist_hbm, ham_ref, out_ref, norm_ref,
    row, hist, r_high, r_low, r_ham, left, l_ham, cx, rx, sx, zs, rz, win,
    part, rc, sc, ry, slope, pred, norm_p, norm_x, norm_z,
    in_sem, x_sem, a_sem, z_sem, gz_sem, gx_sem, c_send, c_recv, y_send, y_recv,
    oy_send, oy_recv, oc_send, oc_recv, n_sem,
):
    n_past, n_x, n_z, chunks, slots, tiles, groups, norm_scale, entries = dims
    n_y = n_past // 2
    size = tiles // groups
    half = LANES // 2
    q, sec = lax.axis_index("past"), lax.axis_index("second")
    z, x = sec // n_x, sec % n_x
    y, core = q // 2, q % 2
    mine = z % chunks
    rows = row.shape[2]

    def at_x(x_to):
        return (q, z * n_x + x_to)

    def at_z(z_to):
        return (q, z_to * n_x + x)

    def at_past(past_to):
        return (past_to, sec)

    partner = at_past(2 * y + (1 - core))

    row_copy = pltpu.make_async_copy(row_hbm, row, in_sem.at[0])
    row_copy.start()
    hist_copy = pltpu.make_async_copy(hist_hbm, hist, in_sem.at[1])
    hist_copy.start()

    barrier = pltpu.get_barrier_semaphore()
    others = [at_x((x + d) % n_x) for d in range(1, n_x)]
    others += [at_past((q + d) % n_past) for d in range(1, n_past)]
    others += [at_z((z + d) % n_z) for d in range(1, n_z)]
    for other in others:
        pl.semaphore_signal(barrier, inc=1, device_id=other, device_id_type=MESH)

    lane = lax.broadcasted_iota(jnp.int32, (1, LANES), 1)
    real = lane < half
    turn = jnp.where(real, F32(1), F32(-1))

    def swap(values):
        return pltpu.roll(values, half, axis=values.ndim - 1)

    def self_energy(values):
        square = values * values
        return (square + swap(square)) * values * F32(-COUPLING)


    def scatter_x(k):
        for d in range(1, n_x):
            to = (x + d) % n_x
            send(cx.at[k, to], rx.at[k, d - 1], x_sem.at[k, 0], x_sem.at[k, 1], at_x(to))

    def sum_x(k):
        wait_bytes(rx.at[k], x_sem.at[k, 1])
        total = cx[k, x]
        for d in range(n_x - 1):
            total = total + rx[k, d]
        return total

    def scatter_z(k):
        for d in range(1, n_z):
            to = (z + d) % n_z
            send(zs.at[k, to % chunks], rz.at[k, d - 1], z_sem.at[k, 0], z_sem.at[k, 1], at_z(to))

    def gather_z(k):
        wait_bytes(rz.at[k], z_sem.at[k, 1])
        total = zs[k, mine]
        for d in range(n_z - 1):
            total = total + rz[k, d]
        win[k, x, mine] = total
        for e in range(1 - chunks // 2, chunks // 2 + 1):
            if e != 0:
                block = win.at[k, x, mine]
                send(block, block, gz_sem.at[k, 0], gz_sem.at[k, 1], at_z((z + e + n_z) % n_z))

    def gather_x(k):
        wait_bytes(win.at[k, 0, pl.ds(0, chunks - 1)], gz_sem.at[k, 1])
        for d in range(1, n_x):
            block = win.at[k, x]
            send(block, block, gx_sem.at[k, 0], gx_sem.at[k, 1], at_x((x + d) % n_x))

    def window_done(k):
        wait_bytes(win.at[k, pl.ds(0, n_x - 1)], gx_sem.at[k, 1])


    def prepare_hist(first, last):
        def body(s, carry):
            columns = pl.ds(pl.multiple_of(s * LANES, LANES), LANES)
            for p in range(slots):
                tile = hist[p, s]
                for kind, values in enumerate((tile, self_energy(tile))):
                    high, low = split(values)
                    at = pl.ds((2 * p + kind) * half, half)
                    r_high[at, columns] = high.astype(BF16)
                    r_low[at, columns] = low.astype(BF16)
            return carry

        lax.fori_loop(first, last, body, 0)

    def prepare_ham():
        tile = ham_ref[...]
        flipped = jnp.concatenate([tile, jnp.zeros_like(tile)], axis=0).T
        ham = F32(0.5) * (tile * turn + flipped[:half] + swap(flipped[half:]))
        slope[pl.ds(0, n_past)] = ham.reshape(n_past, rows, LANES)

    def prepare_left_ham():
        high, low = split(slope[q])
        blank = jnp.zeros((LANES - 3 * rows, LANES), F32)
        l_ham[...] = jnp.concatenate([high, high, low, blank], axis=0).T.astype(BF16)
        r_ham[...] = jnp.zeros(r_ham.shape, BF16)

    def prepare_right_ham(s, values):
        high, low = split(values)
        both = jnp.concatenate([high, low, high, jnp.zeros_like(high)], axis=0)
        r_ham[pl.ds(0, 4 * rows), pl.ds(s * LANES, LANES)] = both.astype(BF16)

    def prepare_left(k):
        for t in range(slots):
            weight = table_ref[index_ref[t]] * F32(norm_scale)
            tile = win[k, t].reshape(half, LANES)
            first = weight * self_energy(tile)
            second = weight * tile
            real_part = jnp.where(real, first, swap(second))
            imag_part = jnp.where(real, swap(first), second)
            high, low = split(jnp.concatenate([real_part, imag_part], axis=0))
            left[pl.ds(0, LANES), pl.ds(t * LANES, LANES)] = high.astype(BF16)
            left[pl.ds(LANES, LANES), pl.ds(t * LANES, LANES)] = low.astype(BF16)

    def contract(k, g):
        columns = pl.ds(g * size * LANES, size * LANES)
        both = jnp.dot(left[...], r_high[:, columns], preferred_element_type=F32)
        more = jnp.dot(left[pl.ds(0, LANES), :], r_low[:, columns], preferred_element_type=F32)
        ham = jnp.dot(l_ham[...], r_ham[:, columns], preferred_element_type=F32)
        total = both[:LANES] + both[LANES:] + more + ham
        for s in range(size):
            at = slice(s * LANES, (s + 1) * LANES)
            tile = total[:half, at] - turn * swap(total[half:, at])
            for p in range(n_past):
                part[k, g, p % 2, p // 2, s] = tile[p * rows : (p + 1) * rows]
        send(part.at[k, g, 1 - core], rc.at[k, g], c_send.at[k, g], c_recv.at[k, g], partner)

    def between_chips(k, g):
        wait_bytes(rc.at[k, g], c_recv.at[k, g])
        sc[k, g] = part[k, g, core] + rc[k, g]
        for d in range(1, n_y):
            to = (y + d) % n_y
            send(sc.at[k, g, to], ry.at[k, g, d - 1], y_send.at[k, g], y_recv.at[k, g], at_past(2 * to + core))

    def slope_of(k, g):
        wait_bytes(ry.at[k, g], y_recv.at[k, g])
        total = sc[k, g, y]
        for d in range(n_y - 1):
            total = total + ry[k, g, d]
        return turn * swap(total.reshape(size * rows, LANES)).reshape(size, rows, LANES)

    def run(k, finish):
        for g in range(groups + 2):
            if g < groups:
                contract(k, g)
            if 0 <= g - 1 < groups:
                between_chips(k, g - 1)
            if 0 <= g - 2 < groups:
                finish(g - 2, slope_of(k, g - 2))


    start = start_ref[0]
    row_copy.wait()
    for t in range(slots):
        wanted = start + slots * q + t - tiles * sec
        inside = (wanted >= 0) & (wanted < tiles)
        tile = row[jnp.clip(wanted, 0, tiles - 1)]
        cx[0, t] = jnp.where(inside, tile, jnp.zeros_like(tile))
    pl.semaphore_wait(barrier, len(others))
    scatter_x(0)
    prepare_ham()
    prepare_left_ham()
    for s in range(tiles):
        prepare_right_ham(s, row[s, q])
    zs[0] = sum_x(0).reshape(zs.shape[1:])
    scatter_z(0)
    hist_copy.wait()
    prepare_hist(0, tiles // 2)
    gather_z(0)
    prepare_hist(tiles // 2, tiles)
    gather_x(0)
    window_done(0)
    prepare_left(0)

    def finish_first(g, values):
        for i in range(size):
            s = g * size + i
            slope[s] = values[i]
            ahead = row[s, q] + F32(STEP) * values[i]
            pred[s] = ahead

    run(0, finish_first)


    for p in range(slots * n_past):
        wanted = start + p - tiles * sec
        inside = (wanted >= 0) & (wanted < tiles)
        tile = pred[jnp.clip(wanted, 0, tiles - 1)]
        cx[1, p % slots, p // slots] = jnp.where(inside, tile, jnp.zeros_like(tile))
    scatter_x(1)
    for s in range(tiles):
        prepare_right_ham(s, pred[s])
    sx[...] = sum_x(1)
    for d in range(1, n_past):
        to = (q + d) % n_past
        send(sx.at[to], zs.at[1, q], a_sem.at[0], a_sem.at[1], at_past(to))
    zs[1, q] = sx[q]
    wait_bytes(zs.at[1, pl.ds(0, n_past - 1)], a_sem.at[1])
    scatter_z(1)
    gather_z(1)
    gather_x(1)
    window_done(1)
    prepare_left(1)

    def to_chips(g, values):
        squares = jnp.zeros((rows, LANES), F32)
        for i in range(size):
            s = g * size + i
            after = row[s, q] + F32(0.5 * STEP) * (slope[s] + values[i])
            out_ref[s, y, core] = after
            change = after - pred[s]
            squares = squares + change * change
        norm_p[q] = (norm_p[q] if g else 0) + jnp.sum(squares, axis=0, keepdims=True)
        block = out_ref.at[pl.ds(g * size, size), y, core]
        for d in range(1, n_y):
            send(block, block, oy_send.at[g], oy_recv.at[g], at_past(2 * ((y + d) % n_y) + core))

    run(1, to_chips)

    def share(buffer, own, number, n, where):
        for d in range(1, n):
            block = buffer.at[own]
            send(block, block, n_sem.at[number, 0], n_sem.at[number, 1], where((own + d) % n))

    def shared(buffer, number, n):
        wait_bytes(buffer.at[pl.ds(0, n - 1)], n_sem.at[number, 1])
        total = buffer[0]
        for i in range(1, n):
            total = total + buffer[i]
        return total

    share(norm_p, q, 0, n_past, at_past)
    for g in range(groups):
        wait_bytes(rc.at[0, g, pl.ds(0, n_y - 1)], oy_recv.at[g])
        block = out_ref.at[pl.ds(g * size, size), :, core]
        send(block, block, oc_send.at[g], oc_recv.at[g], partner)
    norm_x[x] = shared(norm_p, 0, n_past)
    share(norm_x, x, 1, n_x, at_x)
    norm_z[z] = shared(norm_x, 1, n_x)
    share(norm_z, z, 2, n_z, at_z)
    total = shared(norm_z, 2, n_z)
    mean = jnp.sum(total, axis=1, keepdims=True) * F32(1.0 / entries)
    norm_ref[0] = (jnp.sqrt(jnp.broadcast_to(mean, (1, LANES))) * F32(1.0 / STEP))[0, 0]
    for g in range(groups):
        wait_bytes(rc.at[0, g], oc_recv.at[g])

    for k in range(2):
        wait_bytes(rx.at[k], x_sem.at[k, 0])
        wait_bytes(rz.at[k], z_sem.at[k, 0])
        wait_bytes(win.at[k, 0, pl.ds(0, chunks - 1)], gz_sem.at[k, 0])
        wait_bytes(win.at[k, pl.ds(0, n_x - 1)], gx_sem.at[k, 0])
        for g in range(groups):
            wait_bytes(rc.at[k, g], c_send.at[k, g])
            wait_bytes(ry.at[k, g], y_send.at[k, g])
    for g in range(groups):
        wait_bytes(rc.at[0, g, pl.ds(0, n_y - 1)], oy_send.at[g])
        wait_bytes(rc.at[0, g], oc_send.at[g])
    wait_bytes(zs.at[1, pl.ds(0, n_past - 1)], a_sem.at[0])
    wait_bytes(norm_p.at[pl.ds(0, n_past - 1)], n_sem.at[0, 0])
    wait_bytes(norm_x.at[pl.ds(0, n_x - 1)], n_sem.at[1, 0])
    wait_bytes(norm_z.at[pl.ds(0, n_z - 1)], n_sem.at[2, 0])


def local(n_past, n_second, green_row, green_hist, hamiltonian, quad_table, weight_index, block_start):
    tiles, orbits, _ = green_row.shape
    slots = green_hist.shape[0]
    n_x = CHIPS_X
    n_z = n_second // n_x
    n_y = n_past // 2
    rows = orbits // n_past
    chunks = n_past
    groups = 4 if tiles % 4 == 0 and tiles > 4 else 2
    size = tiles // groups
    depth = 2 * slots * orbits
    dims = (
        n_past, n_x, n_z, chunks, slots, tiles, groups,
        1.0 / math.sqrt(orbits * slots * n_past), tiles * n_second * orbits * 2 * orbits,
    )
    dma = pltpu.SemaphoreType.DMA
    scratch = [
        pltpu.VMEM((tiles, n_past, rows, LANES), F32),
        pltpu.VMEM((slots, tiles, orbits, LANES), F32),
        pltpu.VMEM((depth, tiles * LANES), BF16),
        pltpu.VMEM((depth, tiles * LANES), BF16),
        pltpu.VMEM((LANES, tiles * LANES), BF16),
        pltpu.VMEM((2 * LANES, depth), BF16),
        pltpu.VMEM((LANES, LANES), BF16),
        pltpu.VMEM((2, n_x, n_past, rows, LANES), F32),
        pltpu.VMEM((2, n_x - 1, n_past, rows, LANES), F32),
        pltpu.VMEM((n_past, rows, LANES), F32),
        pltpu.VMEM((2, chunks, rows, LANES), F32),
        pltpu.VMEM((2, n_z - 1, rows, LANES), F32),
        pltpu.VMEM((2, slots, chunks, rows, LANES), F32),
        pltpu.VMEM((2, groups, 2, n_y, size, rows, LANES), F32),
        pltpu.VMEM((2, groups, n_y, size, rows, LANES), F32),
        pltpu.VMEM((2, groups, n_y, size, rows, LANES), F32),
        pltpu.VMEM((2, groups, n_y - 1, size, rows, LANES), F32),
        pltpu.VMEM((max(tiles, n_past), rows, LANES), F32),
        pltpu.VMEM((tiles, rows, LANES), F32),
        pltpu.VMEM((n_past, 1, LANES), F32),
        pltpu.VMEM((n_x, 1, LANES), F32),
        pltpu.VMEM((n_z, 1, LANES), F32),
        dma((2,)),
        dma((2, 2)),
        dma((2,)),
        dma((2, 2)),
        dma((2, 2)),
        dma((2, 2)),
        dma((2, groups)), dma((2, groups)),
        dma((2, groups)), dma((2, groups)),
        dma((groups,)), dma((groups,)),
        dma((groups,)), dma((groups,)),
        dma((3, 2)),
    ]
    smem = pl.BlockSpec(memory_space=pltpu.SMEM)
    vmem = pl.BlockSpec(memory_space=pltpu.VMEM)
    anywhere = pl.BlockSpec(memory_space=pl.ANY)
    after, change = pl.pallas_call(
        functools.partial(kernel, dims),
        out_shape=(
            jax.ShapeDtypeStruct((tiles, n_y, 2, rows, LANES), F32),
            jax.ShapeDtypeStruct((1,), F32),
        ),
        in_specs=[smem, smem, smem, anywhere, anywhere, vmem],
        out_specs=(vmem, smem),
        scratch_shapes=scratch,
        compiler_params=pltpu.CompilerParams(
            collective_id=0, has_side_effects=True, vmem_limit_bytes=40 * 1024 * 1024
        ),
    )(
        block_start, weight_index, quad_table,
        green_row.reshape(tiles, n_past, rows, LANES), green_hist, hamiltonian,
    )
    return after.reshape(tiles, orbits, LANES), change


def solution(mesh):
    placed = (P("second", None, None), P("past", "second", None, None), P(), P(), P("past"), P())
    return jax.shard_map(
        functools.partial(local, mesh.shape["past"], mesh.shape["second"]),
        mesh=mesh,
        in_specs=placed,
        out_specs=(P("second", None, None), P()),
        check_vma=False,
    )
```

```python
import functools
import math

import jax
import jax.numpy as jnp
from jax import lax
from jax.experimental import pallas as pl
from jax.experimental.pallas import tpu as pltpu
from jax.sharding import PartitionSpec as P

COUPLING = 0.5
STEP = 0.25
CHIPS_X = 4
LANES = 128
MESH = pl.DeviceIdType.MESH
F32 = jnp.float32
BF16 = jnp.bfloat16


def wait_bytes(ref, sem):
    pltpu.make_async_copy(ref, ref, sem).wait()


def send(src, dst, send_sem, recv_sem, where):
    pltpu.make_async_remote_copy(
        src_ref=src, dst_ref=dst, send_sem=send_sem, recv_sem=recv_sem, device_id=where, device_id_type=MESH
    ).start()


def far_first(n):
    return sorted(range(1, n), key=lambda d: -min(d, n - d))


def split(values):
    high = values.astype(BF16).astype(F32)
    return high, values - high


def kernel(
    dims, start_ref, index_ref, table_ref, row_hbm, hist_hbm, ham_ref, out_ref, norm_ref,
    row, hist, r_high, r_low, r_ham, left, l_ham, cx, rx, rp, zs, rz, win,
    part, rc, sc, ry, slope, pred, norm_p, norm_z,
    in_sem, x_sem, a_sem, z_sem, g_sem, c_send, c_recv, y_send, y_recv,
    oy_send, oy_recv, oc_send, oc_recv, n_sem,
):
    n_past, n_x, n_z, chunks, slots, tiles, groups, norm_scale, entries = dims
    n_y = n_past // 2
    size = tiles // groups
    half = LANES // 2
    q, sec = lax.axis_index("past"), lax.axis_index("second")
    z, x = sec // n_x, sec % n_x
    y, core = q // 2, q % 2
    mine = z % chunks
    rows = row.shape[2]

    def at_x(x_to):
        return (q, z * n_x + x_to)

    def at_z(z_to):
        return (q, z_to * n_x + x)

    def at_past(past_to):
        return (past_to, sec)

    def at_plane(d):
        return (2 * ((y + d[0]) % n_y) + (core + d[1]) % 2, z * n_x + (x + d[2]) % n_x)

    plane = [(a, b, c) for a in range(n_y) for b in range(2) for c in range(n_x)][1:]
    plane.sort(key=lambda d: -min(d[0], n_y - d[0]) - min(d[2], n_x - d[2]))
    partner = at_past(2 * y + (1 - core))

    row_copy = pltpu.make_async_copy(row_hbm, row, in_sem.at[0])
    row_copy.start()
    hist_copy = pltpu.make_async_copy(hist_hbm, hist, in_sem.at[1])
    hist_copy.start()

    barrier = pltpu.get_barrier_semaphore()
    reach = min(chunks // 2, n_z // 2)
    others = [at_z((z + d) % n_z) for d in far_first(n_z)]
    others += [
        (q, (z + e) % n_z * n_x + (x + d) % n_x)
        for e in far_first(n_z)
        if min(e, n_z - e) <= reach
        for d in range(1, n_x)
    ]
    others += [at_plane(d) for d in plane]
    for other in others:
        pl.semaphore_signal(barrier, inc=1, device_id=other, device_id_type=MESH)

    lane = lax.broadcasted_iota(jnp.int32, (1, LANES), 1)
    real = lane < half
    turn = jnp.where(real, F32(1), F32(-1))

    def swap(values):
        return pltpu.roll(values, half, axis=values.ndim - 1)

    def self_energy(values):
        square = values * values
        return (square + swap(square)) * values * F32(-COUPLING)


    def scatter_x():
        for d in far_first(n_x):
            to = (x + d) % n_x
            send(cx.at[0, to], rx.at[d - 1], x_sem.at[0], x_sem.at[1], at_x(to))

    def sum_x():
        wait_bytes(rx, x_sem.at[1])
        total = cx[0, x]
        for d in range(n_x - 1):
            total = total + rx[d]
        return total

    def scatter_plane():
        for d in plane:
            to, column = at_plane(d)
            block = cx.at[1, column % n_x, to]
            send(block, rp.at[x * n_past + q], a_sem.at[0], a_sem.at[1], (to, column))
        rp[x * n_past + q] = cx[1, x, q]

    def sum_plane():
        wait_bytes(rp.at[pl.ds(0, n_x * n_past - 1)], a_sem.at[1])
        total = rp[pl.ds(0, n_past)]
        for i in range(1, n_x):
            total = total + rp[pl.ds(i * n_past, n_past)]
        return total

    def scatter_z(k):
        for d in far_first(n_z):
            to = (z + d) % n_z
            send(zs.at[k, to % chunks], rz.at[k, d - 1], z_sem.at[k, 0], z_sem.at[k, 1], at_z(to))

    def gather(k):
        wait_bytes(rz.at[k], z_sem.at[k, 1])
        total = zs[k, mine]
        for d in range(n_z - 1):
            total = total + rz[k, d]
        win[k, x * chunks + mine] = total
        block = win.at[k, x * chunks + mine]
        for e in sorted(range(1 - chunks // 2, chunks // 2 + 1), key=lambda e: -abs(e)):
            for d in far_first(n_x) + [0]:
                if d or e:
                    where = (q, (z + e + n_z) % n_z * n_x + (x + d) % n_x)
                    send(block, block, g_sem.at[k, 0], g_sem.at[k, 1], where)

    def window_done(k):
        wait_bytes(win.at[k, pl.ds(0, slots * chunks - 1)], g_sem.at[k, 1])


    def prepare_hist(first, last):
        def body(s, carry):
            columns = pl.ds(pl.multiple_of(s * LANES, LANES), LANES)
            for p in range(slots):
                tile = hist[p, s]
                for kind, values in enumerate((tile, self_energy(tile))):
                    high, low = split(values)
                    at = pl.ds((2 * p + kind) * half, half)
                    r_high[at, columns] = high.astype(BF16)
                    r_low[at, columns] = low.astype(BF16)
            return carry

        lax.fori_loop(first, last, body, 0)

    def prepare_ham():
        tile = ham_ref[...]
        flipped = jnp.concatenate([tile, jnp.zeros_like(tile)], axis=0).T
        ham = F32(0.5) * (tile * turn + flipped[:half] + swap(flipped[half:]))
        slope[pl.ds(0, n_past)] = ham.reshape(n_past, rows, LANES)

    def prepare_left_ham():
        high, low = split(slope[q])
        blank = jnp.zeros((LANES - 3 * rows, LANES), F32)
        l_ham[...] = jnp.concatenate([high, high, low, blank], axis=0).T.astype(BF16)
        r_ham[...] = jnp.zeros(r_ham.shape, BF16)

    def prepare_right_ham(s, values):
        high, low = split(values)
        both = jnp.concatenate([high, low, high, jnp.zeros_like(high)], axis=0)
        r_ham[pl.ds(0, 4 * rows), pl.ds(s * LANES, LANES)] = both.astype(BF16)

    def prepare_left(k):
        for t in range(slots):
            weight = table_ref[index_ref[t]] * F32(norm_scale)
            tile = win[k, pl.ds(t * chunks, chunks)].reshape(half, LANES)
            first = weight * self_energy(tile)
            second = weight * tile
            real_part = jnp.where(real, first, swap(second))
            imag_part = jnp.where(real, swap(first), second)
            high, low = split(jnp.concatenate([real_part, imag_part], axis=0))
            left[pl.ds(0, LANES), pl.ds(t * LANES, LANES)] = high.astype(BF16)
            left[pl.ds(LANES, LANES), pl.ds(t * LANES, LANES)] = low.astype(BF16)

    def contract(k, g):
        columns = pl.ds(g * size * LANES, size * LANES)
        both = jnp.dot(left[...], r_high[:, columns], preferred_element_type=F32)
        more = jnp.dot(left[pl.ds(0, LANES), :], r_low[:, columns], preferred_element_type=F32)
        ham = jnp.dot(l_ham[...], r_ham[:, columns], preferred_element_type=F32)
        total = both[:LANES] + both[LANES:] + more + ham
        for s in range(size):
            at = slice(s * LANES, (s + 1) * LANES)
            tile = total[:half, at] - turn * swap(total[half:, at])
            for p in range(n_past):
                part[k, g, p % 2, p // 2, s] = tile[p * rows : (p + 1) * rows]
        send(part.at[k, g, 1 - core], rc.at[k, g], c_send.at[k, g], c_recv.at[k, g], partner)

    def between_chips(k, g):
        wait_bytes(rc.at[k, g], c_recv.at[k, g])
        sc[k, g] = part[k, g, core] + rc[k, g]
        for d in far_first(n_y):
            to = (y + d) % n_y
            send(sc.at[k, g, to], ry.at[k, g, d - 1], y_send.at[k, g], y_recv.at[k, g], at_past(2 * to + core))

    def slope_of(k, g):
        wait_bytes(ry.at[k, g], y_recv.at[k, g])
        total = sc[k, g, y]
        for d in range(n_y - 1):
            total = total + ry[k, g, d]
        return turn * swap(total.reshape(size * rows, LANES)).reshape(size, rows, LANES)

    def run(k, finish):
        for g in range(groups + 1):
            if g < groups:
                contract(k, g)
            if g >= 1:
                between_chips(k, g - 1)
        for g in range(groups):
            finish(g, slope_of(k, g))


    start = start_ref[0]
    row_copy.wait()
    for t in range(slots):
        wanted = start + slots * q + t - tiles * sec
        inside = (wanted >= 0) & (wanted < tiles)
        tile = row[jnp.clip(wanted, 0, tiles - 1)]
        cx[0, t] = jnp.where(inside, tile, jnp.zeros_like(tile))
    pl.semaphore_wait(barrier, len(others))
    scatter_x()
    prepare_ham()
    prepare_left_ham()
    for s in range(tiles):
        prepare_right_ham(s, row[s, q])
    zs[0] = sum_x().reshape(zs.shape[1:])
    scatter_z(0)
    hist_copy.wait()
    prepare_hist(0, tiles // 2)
    gather(0)
    prepare_hist(tiles // 2, tiles)
    window_done(0)
    prepare_left(0)

    def finish_first(g, values):
        for i in range(size):
            s = g * size + i
            slope[s] = values[i]
            ahead = row[s, q] + F32(STEP) * values[i]
            pred[s] = ahead

    run(0, finish_first)


    for p in range(slots * n_past):
        wanted = start + p - tiles * sec
        inside = (wanted >= 0) & (wanted < tiles)
        tile = pred[jnp.clip(wanted, 0, tiles - 1)]
        cx[1, p % slots, p // slots] = jnp.where(inside, tile, jnp.zeros_like(tile))
    scatter_plane()
    for s in range(tiles):
        prepare_right_ham(s, pred[s])
    zs[1] = sum_plane()
    scatter_z(1)
    gather(1)
    window_done(1)
    prepare_left(1)

    def to_chips(g, values):
        squares = jnp.zeros((rows, LANES), F32)
        for i in range(size):
            s = g * size + i
            after = row[s, q] + F32(0.5 * STEP) * (slope[s] + values[i])
            out_ref[s, y, core] = after
            change = after - pred[s]
            squares = squares + change * change
        norm_p[x * n_past + q] = (norm_p[x * n_past + q] if g else 0) + jnp.sum(squares, axis=0, keepdims=True)
        block = out_ref.at[pl.ds(g * size, size), y, core]
        for d in far_first(n_y):
            send(block, block, oy_send.at[g], oy_recv.at[g], at_past(2 * ((y + d) % n_y) + core))

    run(1, to_chips)

    def shared(buffer, number, n):
        wait_bytes(buffer.at[pl.ds(0, n - 1)], n_sem.at[number, 1])
        total = buffer[0]
        for i in range(1, n):
            total = total + buffer[i]
        return total

    block = norm_p.at[x * n_past + q]
    for d in plane:
        send(block, block, n_sem.at[0, 0], n_sem.at[0, 1], at_plane(d))
    for g in range(groups):
        wait_bytes(rc.at[0, g, pl.ds(0, n_y - 1)], oy_recv.at[g])
        block = out_ref.at[pl.ds(g * size, size), :, core]
        send(block, block, oc_send.at[g], oc_recv.at[g], partner)
    norm_z[z] = shared(norm_p, 0, n_x * n_past)
    block = norm_z.at[z]
    for d in far_first(n_z):
        send(block, block, n_sem.at[1, 0], n_sem.at[1, 1], at_z((z + d) % n_z))
    total = shared(norm_z, 1, n_z)
    mean = jnp.sum(total, axis=1, keepdims=True) * F32(1.0 / entries)
    norm_ref[0] = (jnp.sqrt(jnp.broadcast_to(mean, (1, LANES))) * F32(1.0 / STEP))[0, 0]
    for g in range(groups):
        wait_bytes(rc.at[0, g], oc_recv.at[g])

    wait_bytes(rx, x_sem.at[0])
    wait_bytes(rp.at[pl.ds(0, n_x * n_past - 1)], a_sem.at[0])
    for k in range(2):
        wait_bytes(rz.at[k], z_sem.at[k, 0])
        wait_bytes(win.at[k, pl.ds(0, slots * chunks - 1)], g_sem.at[k, 0])
        for g in range(groups):
            wait_bytes(rc.at[k, g], c_send.at[k, g])
            wait_bytes(ry.at[k, g], y_send.at[k, g])
    for g in range(groups):
        wait_bytes(rc.at[0, g, pl.ds(0, n_y - 1)], oy_send.at[g])
        wait_bytes(rc.at[0, g], oc_send.at[g])
    wait_bytes(norm_p.at[pl.ds(0, n_x * n_past - 1)], n_sem.at[0, 0])
    wait_bytes(norm_z.at[pl.ds(0, n_z - 1)], n_sem.at[1, 0])


def local(n_past, n_second, green_row, green_hist, hamiltonian, quad_table, weight_index, block_start):
    tiles, orbits, _ = green_row.shape
    slots = green_hist.shape[0]
    n_x = CHIPS_X
    n_z = n_second // n_x
    n_y = n_past // 2
    rows = orbits // n_past
    chunks = n_past
    groups = 4 if tiles % 4 == 0 and tiles > 4 else 2
    size = tiles // groups
    depth = 2 * slots * orbits
    dims = (
        n_past, n_x, n_z, chunks, slots, tiles, groups,
        1.0 / math.sqrt(orbits * slots * n_past), tiles * n_second * orbits * 2 * orbits,
    )
    dma = pltpu.SemaphoreType.DMA
    scratch = [
        pltpu.VMEM((tiles, n_past, rows, LANES), F32),
        pltpu.VMEM((slots, tiles, orbits, LANES), F32),
        pltpu.VMEM((depth, tiles * LANES), BF16),
        pltpu.VMEM((depth, tiles * LANES), BF16),
        pltpu.VMEM((LANES, tiles * LANES), BF16),
        pltpu.VMEM((2 * LANES, depth), BF16),
        pltpu.VMEM((LANES, LANES), BF16),
        pltpu.VMEM((2, n_x, n_past, rows, LANES), F32),
        pltpu.VMEM((n_x - 1, n_past, rows, LANES), F32),
        pltpu.VMEM((n_x * n_past, rows, LANES), F32),
        pltpu.VMEM((2, chunks, rows, LANES), F32),
        pltpu.VMEM((2, n_z - 1, rows, LANES), F32),
        pltpu.VMEM((2, slots * chunks, rows, LANES), F32),
        pltpu.VMEM((2, groups, 2, n_y, size, rows, LANES), F32),
        pltpu.VMEM((2, groups, n_y, size, rows, LANES), F32),
        pltpu.VMEM((2, groups, n_y, size, rows, LANES), F32),
        pltpu.VMEM((2, groups, n_y - 1, size, rows, LANES), F32),
        pltpu.VMEM((max(tiles, n_past), rows, LANES), F32),
        pltpu.VMEM((tiles, rows, LANES), F32),
        pltpu.VMEM((n_x * n_past, 1, LANES), F32),
        pltpu.VMEM((n_z, 1, LANES), F32),
        dma((2,)),
        dma((2,)),
        dma((2,)),
        dma((2, 2)),
        dma((2, 2)),
        dma((2, groups)), dma((2, groups)),
        dma((2, groups)), dma((2, groups)),
        dma((groups,)), dma((groups,)),
        dma((groups,)), dma((groups,)),
        dma((2, 2)),
    ]
    smem = pl.BlockSpec(memory_space=pltpu.SMEM)
    vmem = pl.BlockSpec(memory_space=pltpu.VMEM)
    anywhere = pl.BlockSpec(memory_space=pl.ANY)
    after, change = pl.pallas_call(
        functools.partial(kernel, dims),
        out_shape=(
            jax.ShapeDtypeStruct((tiles, n_y, 2, rows, LANES), F32),
            jax.ShapeDtypeStruct((1,), F32),
        ),
        in_specs=[smem, smem, smem, anywhere, anywhere, vmem],
        out_specs=(vmem, smem),
        scratch_shapes=scratch,
        compiler_params=pltpu.CompilerParams(
            collective_id=0, has_side_effects=True, vmem_limit_bytes=60 * 1024 * 1024
        ),
    )(
        block_start, weight_index, quad_table,
        green_row.reshape(tiles, n_past, rows, LANES), green_hist, hamiltonian,
    )
    return after.reshape(tiles, orbits, LANES), change


def solution(mesh):
    placed = (P("second", None, None), P("past", "second", None, None), P(), P(), P("past"), P())
    return jax.shard_map(
        functools.partial(local, mesh.shape["past"], mesh.shape["second"]),
        mesh=mesh,
        in_specs=placed,
        out_specs=(P("second", None, None), P()),
        check_vma=False,
    )
```

```python
import functools
import math

import jax
import jax.numpy as jnp
from jax import lax
from jax.experimental import pallas as pl
from jax.experimental.pallas import tpu as pltpu
from jax.sharding import PartitionSpec as P

COUPLING = 0.5
STEP = 0.25
PRODUCTS = 1
GROUPS = 4
CHIPS_X = 4
LANES = 128
MESH = pl.DeviceIdType.MESH
F32 = jnp.float32
BF16 = jnp.bfloat16


def wait_bytes(ref, sem):
    pltpu.make_async_copy(ref, ref, sem).wait()


def send(src, dst, send_sem, recv_sem, where):
    pltpu.make_async_remote_copy(
        src_ref=src, dst_ref=dst, send_sem=send_sem, recv_sem=recv_sem, device_id=where, device_id_type=MESH
    ).start()


def far_first(n):
    return sorted(range(1, n), key=lambda d: -min(d, n - d))


def split(values):
    high = values.astype(BF16).astype(F32)
    return high, values - high


def kernel(
    dims, start_ref, index_hbm, table_hbm, row_hbm, hist_hbm, ham_hbm, out_hbm, norm_ref,
    index_ref, table_ref, row, hist, ham_ref, near, early, r_high, r_low, r_ham, left, l_ham, cx, rx, rp, zs, rz, win,
    part, rc, sc, ry, slope, pred, norm_p, norm_z, out,
    in_sem, x_sem, near_sem, a_sem, z_sem, g_sem, c_send, c_recv, y_send, y_recv,
    oy_send, oy_recv, oc_send, oc_recv, n_sem, out_sem,
):
    n_past, n_x, n_z, chunks, slots, tiles, groups, norm_scale, entries = dims
    n_y = n_past // 2
    size = tiles // groups
    half = LANES // 2
    q, sec = lax.axis_index("past"), lax.axis_index("second")
    z, x = sec // n_x, sec % n_x
    y, core = q // 2, q % 2
    mine = z % chunks
    rows = row.shape[2]

    def at_x(x_to):
        return (q, z * n_x + x_to)

    def at_z(z_to):
        return (q, z_to * n_x + x)

    def at_past(past_to):
        return (past_to, sec)

    def at_plane(d):
        return (2 * ((y + d[0]) % n_y) + (core + d[1]) % 2, z * n_x + (x + d[2]) % n_x)

    plane = [(a, b, c) for a in range(n_y) for b in range(2) for c in range(n_x)][1:]
    plane.sort(key=lambda d: -min(d[0], n_y - d[0]) - min(d[2], n_x - d[2]))
    partner = at_past(2 * y + (1 - core))

    copies = []
    for source, target in (
        (row_hbm, row), (hist_hbm, hist), (ham_hbm, ham_ref),
        (index_hbm, index_ref), (table_hbm, table_ref),
    ):
        copies.append(pltpu.make_async_copy(source, target, in_sem.at[len(copies)]))

    barrier = pltpu.get_barrier_semaphore()
    reach = min(chunks // 2, n_z // 2)
    others = [at_z((z + d) % n_z) for d in far_first(n_z)]
    others += [
        (q, (z + e) % n_z * n_x + (x + d) % n_x)
        for e in far_first(n_z)
        if min(e, n_z - e) <= reach
        for d in range(1, n_x)
    ]
    others += [at_plane(d) for d in plane]
    for other in others:
        pl.semaphore_signal(barrier, inc=1, device_id=other, device_id_type=MESH)

    for copy in copies:
        copy.start()

    lane = lax.broadcasted_iota(jnp.int32, (1, LANES), 1)
    real = lane < half
    turn = jnp.where(real, F32(1), F32(-1))

    def swap(values):
        return pltpu.roll(values, half, axis=values.ndim - 1)

    def self_energy(values):
        square = values * values
        return (square + swap(square)) * values * F32(-COUPLING)


    def scatter_x():
        for d in far_first(n_x):
            to = (x + d) % n_x
            send(cx.at[0, to], rx.at[d - 1], x_sem.at[0], x_sem.at[1], at_x(to))

    def sum_x():
        wait_bytes(rx, x_sem.at[1])
        total = cx[0, x]
        for d in range(n_x - 1):
            total = total + rx[d]
        return total

    def scatter_plane():
        for d in plane:
            to, column = at_plane(d)
            block = cx.at[1, column % n_x, to]
            send(block, rp.at[x * n_past + q], a_sem.at[0], a_sem.at[1], (to, column))
        rp[x * n_past + q] = cx[1, x, q]

    def sum_plane():
        wait_bytes(rp.at[pl.ds(0, n_x * n_past - 1)], a_sem.at[1])
        total = rp[pl.ds(0, n_past)]
        for i in range(1, n_x):
            total = total + rp[pl.ds(i * n_past, n_past)]
        return total

    def spread_near():
        for e in (1, n_z - 1, 0):
            for d in far_first(n_x) + [0]:
                if d or e:
                    slot = (0 if e == 0 else 1 if e == 1 else 2) * n_x + x
                    where = (q, (z + e) % n_z * n_x + (x + d) % n_x)
                    send(zs.at[0], near.at[slot], near_sem.at[0], near_sem.at[1], where)
        near[x] = zs[0]

    def near_done():
        wait_bytes(near.at[pl.ds(0, 3 * n_x - 1)], near_sem.at[1])

    def near_tile(t):
        return (near[t] + near[n_x + t] + near[2 * n_x + t]).reshape(half, LANES)

    def scatter_z(k):
        for d in far_first(n_z):
            to = (z + d) % n_z
            send(zs.at[k, to % chunks], rz.at[k, d - 1], z_sem.at[k, 0], z_sem.at[k, 1], at_z(to))

    def gather(k):
        wait_bytes(rz.at[k], z_sem.at[k, 1])
        total = zs[k, mine]
        for d in range(n_z - 1):
            total = total + rz[k, d]
        win[k, x * chunks + mine] = total
        block = win.at[k, x * chunks + mine]
        for e in sorted(range(1 - chunks // 2, chunks // 2 + 1), key=lambda e: -abs(e)):
            for d in far_first(n_x) + [0]:
                if d or e:
                    where = (q, (z + e + n_z) % n_z * n_x + (x + d) % n_x)
                    send(block, block, g_sem.at[k, 0], g_sem.at[k, 1], where)

    def window_done(k):
        wait_bytes(win.at[k, pl.ds(0, slots * chunks - 1)], g_sem.at[k, 1])

    def window_tile(k):
        return lambda t: win[k, pl.ds(t * chunks, chunks)].reshape(half, LANES)


    def prepare_hist(first, last):
        def body(s, carry):
            columns = pl.ds(pl.multiple_of(s * LANES, LANES), LANES)
            for p in range(slots):
                tile = hist[p, s]
                for kind, values in enumerate((tile, self_energy(tile))):
                    high, low = split(values)
                    at = pl.ds((2 * p + kind) * half, half)
                    r_high[at, columns] = high.astype(BF16)
                    r_low[at, columns] = low.astype(BF16)
            return carry

        lax.fori_loop(first, last, body, 0)

    def prepare_ham():
        tile = ham_ref[...]
        flipped = jnp.concatenate([tile, jnp.zeros_like(tile)], axis=0).T
        ham = F32(0.5) * (tile * turn + flipped[:half] + swap(flipped[half:]))
        slope[pl.ds(0, n_past)] = ham.reshape(n_past, rows, LANES)

    def prepare_left_ham():
        high, low = split(slope[q])
        blank = jnp.zeros((LANES - 3 * rows, LANES), F32)
        l_ham[...] = jnp.concatenate([high, high, low, blank], axis=0).T.astype(BF16)
        r_ham[...] = jnp.zeros(r_ham.shape, BF16)

    def prepare_right_ham(s, values):
        high, low = split(values)
        both = jnp.concatenate([high, low, high, jnp.zeros_like(high)], axis=0)
        r_ham[pl.ds(0, 4 * rows), pl.ds(s * LANES, LANES)] = both.astype(BF16)

    def prepare_left(tile_of):
        for t in range(slots):
            weight = table_ref[index_ref[t]] * F32(norm_scale)
            tile = tile_of(t)
            first = weight * self_energy(tile)
            second = weight * tile
            real_part = jnp.where(real, first, swap(second))
            imag_part = jnp.where(real, swap(first), second)
            high, low = split(jnp.concatenate([real_part, imag_part], axis=0))
            left[pl.ds(0, LANES), pl.ds(t * LANES, LANES)] = high.astype(BF16)
            left[pl.ds(LANES, LANES), pl.ds(t * LANES, LANES)] = low.astype(BF16)

    def contract(k, number):
        wide = tiles // PRODUCTS
        columns = pl.ds(number * wide * LANES, wide * LANES)
        both = jnp.dot(left[...], r_high[:, columns], preferred_element_type=F32)
        more = jnp.dot(left[pl.ds(0, LANES), :], r_low[:, columns], preferred_element_type=F32)
        ham = jnp.dot(l_ham[...], r_ham[:, columns], preferred_element_type=F32)
        total = both[:LANES] + both[LANES:] + more + ham
        for i in range(wide):
            at = slice(i * LANES, (i + 1) * LANES)
            tile = total[:half, at] - turn * swap(total[half:, at])
            g, s = divmod(number * wide + i, size)
            for p in range(n_past):
                part[k, g, p % 2, p // 2, s] = tile[p * rows : (p + 1) * rows]
            if s == size - 1:
                send(part.at[k, g, 1 - core], rc.at[k, g], c_send.at[k, g], c_recv.at[k, g], partner)

    def between_chips(k, g):
        wait_bytes(rc.at[k, g], c_recv.at[k, g])
        sc[k, g] = part[k, g, core] + rc[k, g]
        for d in far_first(n_y):
            to = (y + d) % n_y
            send(sc.at[k, g, to], ry.at[k, g, d - 1], y_send.at[k, g], y_recv.at[k, g], at_past(2 * to + core))

    def slope_of(k, g):
        wait_bytes(ry.at[k, g], y_recv.at[k, g])
        total = sc[k, g, y]
        for d in range(n_y - 1):
            total = total + ry[k, g, d]
        return turn * swap(total.reshape(size * rows, LANES)).reshape(size, rows, LANES)

    def integrate(k):
        for number in range(PRODUCTS):
            contract(k, number)
        for g in range(groups):
            between_chips(k, g)

    def finish(k, use):
        for g in range(groups):
            use(g, slope_of(k, g))


    start = start_ref[0]
    copies[0].wait()
    for t in range(slots):
        wanted = start + slots * q + t - tiles * sec
        inside = (wanted >= 0) & (wanted < tiles)
        tile = row[jnp.clip(wanted, 0, tiles - 1)]
        cx[0, t] = jnp.where(inside, tile, jnp.zeros_like(tile))
    pl.semaphore_wait(barrier, len(others))
    scatter_x()
    copies[2].wait()
    prepare_ham()
    prepare_left_ham()
    for s in range(tiles):
        prepare_right_ham(s, row[s, q])
    copies[1].wait()
    prepare_hist(0, tiles)
    zs[0] = sum_x().reshape(zs.shape[1:])
    spread_near()
    scatter_z(0)
    copies[3].wait()
    copies[4].wait()
    near_done()
    prepare_left(near_tile)


    def use_near(g, values):
        for i in range(size):
            s = g * size + i
            early[s] = row[s, q] + F32(STEP) * values[i]

    def use_first(g, values):
        for i in range(size):
            s = g * size + i
            slope[s] = values[i]
            pred[s] = row[s, q] + F32(STEP) * values[i]

    integrate(0)
    gather(0)
    finish(0, use_near)


    for p in range(slots * n_past):
        wanted = start + p - tiles * sec
        inside = (wanted >= 0) & (wanted < tiles)
        tile = early[jnp.clip(wanted, 0, tiles - 1)]
        cx[1, p % slots, p // slots] = jnp.where(inside, tile, jnp.zeros_like(tile))
    scatter_plane()
    zs[1] = sum_plane()
    scatter_z(1)
    window_done(0)
    prepare_left(window_tile(0))
    integrate(1)
    gather(1)
    finish(1, use_first)
    for s in range(tiles):
        prepare_right_ham(s, pred[s])
    window_done(1)
    prepare_left(window_tile(1))
    integrate(2)

    def to_chips(g, values):
        squares = jnp.zeros((rows, LANES), F32)
        for i in range(size):
            s = g * size + i
            after = row[s, q] + F32(0.5 * STEP) * (slope[s] + values[i])
            out[s, y, core] = after
            change = after - pred[s]
            squares = squares + change * change
        norm_p[x * n_past + q] = (norm_p[x * n_past + q] if g else 0) + jnp.sum(squares, axis=0, keepdims=True)
        block = out.at[pl.ds(g * size, size), y, core]
        for d in far_first(n_y):
            send(block, block, oy_send.at[g], oy_recv.at[g], at_past(2 * ((y + d) % n_y) + core))

    finish(2, to_chips)

    def shared(buffer, number, n):
        wait_bytes(buffer.at[pl.ds(0, n - 1)], n_sem.at[number, 1])
        total = buffer[0]
        for i in range(1, n):
            total = total + buffer[i]
        return total

    block = norm_p.at[x * n_past + q]
    for d in plane:
        send(block, block, n_sem.at[0, 0], n_sem.at[0, 1], at_plane(d))
    for g in range(groups):
        wait_bytes(rc.at[0, g, pl.ds(0, n_y - 1)], oy_recv.at[g])
        block = out.at[pl.ds(g * size, size), :, core]
        send(block, block, oc_send.at[g], oc_recv.at[g], partner)
    norm_z[z] = shared(norm_p, 0, n_x * n_past)
    block = norm_z.at[z]
    for d in far_first(n_z):
        send(block, block, n_sem.at[1, 0], n_sem.at[1, 1], at_z((z + d) % n_z))
    results = []
    for g in range(groups):
        wait_bytes(rc.at[0, g], oc_recv.at[g])
        block = pl.ds(g * size, size)
        results.append(pltpu.make_async_copy(out.at[block], out_hbm.at[block], out_sem.at[g]))
        results[-1].start()
    total = shared(norm_z, 1, n_z)
    mean = jnp.sum(total, axis=1, keepdims=True) * F32(1.0 / entries)
    norm_ref[0] = (jnp.sqrt(jnp.broadcast_to(mean, (1, LANES))) * F32(1.0 / STEP))[0, 0]
    for result in results:
        result.wait()

    wait_bytes(rx, x_sem.at[0])
    wait_bytes(near.at[pl.ds(0, 3 * n_x - 1)], near_sem.at[0])
    wait_bytes(rp.at[pl.ds(0, n_x * n_past - 1)], a_sem.at[0])
    for k in range(2):
        wait_bytes(rz.at[k], z_sem.at[k, 0])
        wait_bytes(win.at[k, pl.ds(0, slots * chunks - 1)], g_sem.at[k, 0])
    for k in range(3):
        for g in range(groups):
            wait_bytes(rc.at[k, g], c_send.at[k, g])
            wait_bytes(ry.at[k, g], y_send.at[k, g])
    for g in range(groups):
        wait_bytes(rc.at[0, g, pl.ds(0, n_y - 1)], oy_send.at[g])
        wait_bytes(rc.at[0, g], oc_send.at[g])
    wait_bytes(norm_p.at[pl.ds(0, n_x * n_past - 1)], n_sem.at[0, 0])
    wait_bytes(norm_z.at[pl.ds(0, n_z - 1)], n_sem.at[1, 0])


def local(n_past, n_second, green_row, green_hist, hamiltonian, quad_table, weight_index, block_start):
    tiles, orbits, _ = green_row.shape
    slots = green_hist.shape[0]
    n_x = CHIPS_X
    n_z = n_second // n_x
    n_y = n_past // 2
    rows = orbits // n_past
    chunks = n_past
    groups = GROUPS if tiles > 4 else 2
    size = tiles // groups
    depth = 2 * slots * orbits
    dims = (
        n_past, n_x, n_z, chunks, slots, tiles, groups,
        1.0 / math.sqrt(orbits * slots * n_past), tiles * n_second * orbits * 2 * orbits,
    )
    dma = pltpu.SemaphoreType.DMA
    scratch = [
        pltpu.SMEM((slots,), jnp.int32),
        pltpu.SMEM(quad_table.shape, F32),
        pltpu.VMEM((tiles, n_past, rows, LANES), F32),
        pltpu.VMEM((slots, tiles, orbits, LANES), F32),
        pltpu.VMEM((orbits, LANES), F32),
        pltpu.VMEM((3 * n_x, chunks, rows, LANES), F32),
        pltpu.VMEM((tiles, rows, LANES), F32),
        pltpu.VMEM((depth, tiles * LANES), BF16),
        pltpu.VMEM((depth, tiles * LANES), BF16),
        pltpu.VMEM((LANES, tiles * LANES), BF16),
        pltpu.VMEM((2 * LANES, depth), BF16),
        pltpu.VMEM((LANES, LANES), BF16),
        pltpu.VMEM((2, n_x, n_past, rows, LANES), F32),
        pltpu.VMEM((n_x - 1, n_past, rows, LANES), F32),
        pltpu.VMEM((n_x * n_past, rows, LANES), F32),
        pltpu.VMEM((2, chunks, rows, LANES), F32),
        pltpu.VMEM((2, n_z - 1, rows, LANES), F32),
        pltpu.VMEM((2, slots * chunks, rows, LANES), F32),
        pltpu.VMEM((3, groups, 2, n_y, size, rows, LANES), F32),
        pltpu.VMEM((3, groups, n_y, size, rows, LANES), F32),
        pltpu.VMEM((3, groups, n_y, size, rows, LANES), F32),
        pltpu.VMEM((3, groups, n_y - 1, size, rows, LANES), F32),
        pltpu.VMEM((max(tiles, n_past), rows, LANES), F32),
        pltpu.VMEM((tiles, rows, LANES), F32),
        pltpu.VMEM((n_x * n_past, 1, LANES), F32),
        pltpu.VMEM((n_z, 1, LANES), F32),
        pltpu.VMEM((tiles, n_y, 2, rows, LANES), F32),
        dma((5,)),
        dma((2,)),
        dma((2,)),
        dma((2,)),
        dma((2, 2)),
        dma((2, 2)),
        dma((3, groups)), dma((3, groups)),
        dma((3, groups)), dma((3, groups)),
        dma((groups,)), dma((groups,)),
        dma((groups,)), dma((groups,)),
        dma((2, 2)),
        dma((groups,)),
    ]
    smem = pl.BlockSpec(memory_space=pltpu.SMEM)
    anywhere = pl.BlockSpec(memory_space=pl.ANY)
    after, change = pl.pallas_call(
        functools.partial(kernel, dims),
        out_shape=(
            jax.ShapeDtypeStruct((tiles, n_y, 2, rows, LANES), F32),
            jax.ShapeDtypeStruct((1,), F32),
        ),
        in_specs=[smem] + [anywhere] * 5,
        out_specs=(anywhere, smem),
        scratch_shapes=scratch,
        compiler_params=pltpu.CompilerParams(
            collective_id=0, has_side_effects=True, vmem_limit_bytes=60 * 1024 * 1024
        ),
    )(
        block_start, weight_index, quad_table,
        green_row.reshape(tiles, n_past, rows, LANES), green_hist, hamiltonian,
    )
    return after.reshape(tiles, orbits, LANES), change


def solution(mesh):
    placed = (P("second", None, None), P("past", "second", None, None), P(), P(), P("past"), P())
    return jax.shard_map(
        functools.partial(local, mesh.shape["past"], mesh.shape["second"]),
        mesh=mesh,
        in_specs=placed,
        out_specs=(P("second", None, None), P()),
        check_vma=False,
    )
```

```python
import functools
import math

import jax
import jax.numpy as jnp
from jax import lax
from jax.experimental import pallas as pl
from jax.experimental.pallas import tpu as pltpu
from jax.sharding import PartitionSpec as P

COUPLING = 0.5
STEP = 0.25
PRODUCTS = 1
GROUPS = 4
CHIPS_X = 4
LANES = 128
MESH = pl.DeviceIdType.MESH
F32 = jnp.float32
BF16 = jnp.bfloat16


def wait_bytes(ref, sem):
    pltpu.make_async_copy(ref, ref, sem).wait()


def send(src, dst, send_sem, recv_sem, where):
    pltpu.make_async_remote_copy(
        src_ref=src, dst_ref=dst, send_sem=send_sem, recv_sem=recv_sem, device_id=where, device_id_type=MESH
    ).start()


def far_first(n):
    return sorted(range(1, n), key=lambda d: -min(d, n - d))


def split(values):
    high = values.astype(BF16).astype(F32)
    return high, values - high


def kernel(
    dims, start_ref, index_hbm, table_hbm, row_hbm, hist_hbm, ham_hbm, out_hbm, norm_ref,
    index_ref, table_ref, row, hist, ham_ref, near, early, r_high, r_low, r_ham, left, l_ham, cx, rx, rp, zs, rz, win,
    part, rc, sc, ry, slope, pred, norm_p, norm_z, out,
    in_sem, x_sem, near_sem, a_sem, z_sem, g_sem, c_send, c_recv, y_send, y_recv,
    oy_send, oy_recv, oc_send, oc_recv, n_sem, out_sem,
):
    n_past, n_x, n_z, chunks, slots, tiles, groups, norm_scale, entries = dims
    n_y = n_past // 2
    size = tiles // groups
    half = LANES // 2
    q, sec = lax.axis_index("past"), lax.axis_index("second")
    z, x = sec // n_x, sec % n_x
    y, core = q // 2, q % 2
    mine = z % chunks
    rows = row.shape[2]

    def at_x(x_to):
        return (q, z * n_x + x_to)

    def at_z(z_to):
        return (q, z_to * n_x + x)

    def at_past(past_to):
        return (past_to, sec)

    def at_plane(d):
        return (2 * ((y + d[0]) % n_y) + (core + d[1]) % 2, z * n_x + (x + d[2]) % n_x)

    plane = [(a, b, c) for a in range(n_y) for b in range(2) for c in range(n_x)][1:]
    plane.sort(key=lambda d: -min(d[0], n_y - d[0]) - min(d[2], n_x - d[2]))
    partner = at_past(2 * y + (1 - core))

    copies = []
    for source, target in (
        (row_hbm, row), (hist_hbm, hist), (ham_hbm, ham_ref),
        (index_hbm, index_ref), (table_hbm, table_ref),
    ):
        copies.append(pltpu.make_async_copy(source, target, in_sem.at[len(copies)]))

    copies[0].start()
    barrier = pltpu.get_barrier_semaphore()
    reach = min(chunks // 2, n_z // 2)
    others = [at_z((z + d) % n_z) for d in far_first(n_z)]
    others += [
        (q, (z + e) % n_z * n_x + (x + d) % n_x)
        for e in far_first(n_z)
        if min(e, n_z - e) <= reach
        for d in range(1, n_x)
    ]
    others += [at_plane(d) for d in plane]
    for other in others:
        pl.semaphore_signal(barrier, inc=1, device_id=other, device_id_type=MESH)


    lane = lax.broadcasted_iota(jnp.int32, (1, LANES), 1)
    real = lane < half
    turn = jnp.where(real, F32(1), F32(-1))

    def swap(values):
        return pltpu.roll(values, half, axis=values.ndim - 1)

    def self_energy(values):
        square = values * values
        return (square + swap(square)) * values * F32(-COUPLING)


    def scatter_x():
        for d in far_first(n_x):
            to = (x + d) % n_x
            send(cx.at[0, to], rx.at[d - 1], x_sem.at[0], x_sem.at[1], at_x(to))

    def sum_x():
        wait_bytes(rx, x_sem.at[1])
        total = cx[0, x]
        for d in range(n_x - 1):
            total = total + rx[d]
        return total

    def scatter_plane():
        for d in plane:
            to, column = at_plane(d)
            block = cx.at[1, column % n_x, to]
            send(block, rp.at[x * n_past + q], a_sem.at[0], a_sem.at[1], (to, column))
        rp[x * n_past + q] = cx[1, x, q]

    def sum_plane():
        wait_bytes(rp.at[pl.ds(0, n_x * n_past - 1)], a_sem.at[1])
        total = rp[pl.ds(0, n_past)]
        for i in range(1, n_x):
            total = total + rp[pl.ds(i * n_past, n_past)]
        return total

    def spread_near():
        for e in (1, n_z - 1, 0):
            for d in far_first(n_x) + [0]:
                if d or e:
                    slot = (0 if e == 0 else 1 if e == 1 else 2) * n_x + x
                    where = (q, (z + e) % n_z * n_x + (x + d) % n_x)
                    send(zs.at[0], near.at[slot], near_sem.at[0], near_sem.at[1], where)
        near[x] = zs[0]

    def near_done():
        wait_bytes(near.at[pl.ds(0, 3 * n_x - 1)], near_sem.at[1])

    def near_tile(t):
        return (near[t] + near[n_x + t] + near[2 * n_x + t]).reshape(half, LANES)

    def scatter_z(k):
        for d in far_first(n_z):
            to = (z + d) % n_z
            send(zs.at[k, to % chunks], rz.at[k, d - 1], z_sem.at[k, 0], z_sem.at[k, 1], at_z(to))

    def gather(k):
        wait_bytes(rz.at[k], z_sem.at[k, 1])
        total = zs[k, mine]
        for d in range(n_z - 1):
            total = total + rz[k, d]
        win[k, x * chunks + mine] = total
        block = win.at[k, x * chunks + mine]
        for e in sorted(range(1 - chunks // 2, chunks // 2 + 1), key=lambda e: -abs(e)):
            for d in far_first(n_x) + [0]:
                if d or e:
                    where = (q, (z + e + n_z) % n_z * n_x + (x + d) % n_x)
                    send(block, block, g_sem.at[k, 0], g_sem.at[k, 1], where)

    def window_done(k):
        wait_bytes(win.at[k, pl.ds(0, slots * chunks - 1)], g_sem.at[k, 1])

    def window_tile(k):
        return lambda t: win[k, pl.ds(t * chunks, chunks)].reshape(half, LANES)


    def prepare_hist(first, last):
        def body(s, carry):
            columns = pl.ds(pl.multiple_of(s * LANES, LANES), LANES)
            for p in range(slots):
                tile = hist[p, s]
                for kind, values in enumerate((tile, self_energy(tile))):
                    high, low = split(values)
                    at = pl.ds((2 * p + kind) * half, half)
                    r_high[at, columns] = high.astype(BF16)
                    r_low[at, columns] = low.astype(BF16)
            return carry

        lax.fori_loop(first, last, body, 0)

    def prepare_ham():
        tile = ham_ref[...]
        flipped = jnp.concatenate([tile, jnp.zeros_like(tile)], axis=0).T
        ham = F32(0.5) * (tile * turn + flipped[:half] + swap(flipped[half:]))
        slope[pl.ds(0, n_past)] = ham.reshape(n_past, rows, LANES)

    def prepare_left_ham():
        high, low = split(slope[q])
        blank = jnp.zeros((LANES - 3 * rows, LANES), F32)
        l_ham[...] = jnp.concatenate([high, high, low, blank], axis=0).T.astype(BF16)
        r_ham[...] = jnp.zeros(r_ham.shape, BF16)

    def prepare_right_ham(s, values):
        high, low = split(values)
        both = jnp.concatenate([high, low, high, jnp.zeros_like(high)], axis=0)
        r_ham[pl.ds(0, 4 * rows), pl.ds(s * LANES, LANES)] = both.astype(BF16)

    def prepare_left(tile_of):
        for t in range(slots):
            weight = table_ref[index_ref[t]] * F32(norm_scale)
            tile = tile_of(t)
            first = weight * self_energy(tile)
            second = weight * tile
            real_part = jnp.where(real, first, swap(second))
            imag_part = jnp.where(real, swap(first), second)
            high, low = split(jnp.concatenate([real_part, imag_part], axis=0))
            left[pl.ds(0, LANES), pl.ds(t * LANES, LANES)] = high.astype(BF16)
            left[pl.ds(LANES, LANES), pl.ds(t * LANES, LANES)] = low.astype(BF16)

    def contract(k, number):
        wide = tiles // PRODUCTS
        columns = pl.ds(number * wide * LANES, wide * LANES)
        both = jnp.dot(left[...], r_high[:, columns], preferred_element_type=F32)
        more = jnp.dot(left[pl.ds(0, LANES), :], r_low[:, columns], preferred_element_type=F32)
        ham = jnp.dot(l_ham[...], r_ham[:, columns], preferred_element_type=F32)
        total = both[:LANES] + both[LANES:] + more + ham
        for i in range(wide):
            at = slice(i * LANES, (i + 1) * LANES)
            tile = total[:half, at] - turn * swap(total[half:, at])
            g, s = divmod(number * wide + i, size)
            for p in range(n_past):
                part[k, g, p % 2, p // 2, s] = tile[p * rows : (p + 1) * rows]
            if s == size - 1:
                send(part.at[k, g, 1 - core], rc.at[k, g], c_send.at[k, g], c_recv.at[k, g], partner)

    def between_chips(k):
        for g in range(groups):
            wait_bytes(rc.at[k, g], c_recv.at[k, g])
            sc[k, g] = part[k, g, core] + rc[k, g]
        for d in far_first(n_y):
            to = (y + d) % n_y
            for g in range(groups):
                send(sc.at[k, g, to], ry.at[k, g, d - 1], y_send.at[k, g], y_recv.at[k, g], at_past(2 * to + core))

    def slope_of(k, g):
        wait_bytes(ry.at[k, g], y_recv.at[k, g])
        total = sc[k, g, y]
        for d in range(n_y - 1):
            total = total + ry[k, g, d]
        return turn * swap(total.reshape(size * rows, LANES)).reshape(size, rows, LANES)

    def integrate(k):
        for number in range(PRODUCTS):
            contract(k, number)
        between_chips(k)

    def finish(k, use):
        for g in range(groups):
            use(g, slope_of(k, g))


    start = start_ref[0]
    copies[0].wait()
    for copy in copies[1:]:
        copy.start()
    for t in range(slots):
        wanted = start + slots * q + t - tiles * sec
        inside = (wanted >= 0) & (wanted < tiles)
        tile = row[jnp.clip(wanted, 0, tiles - 1)]
        cx[0, t] = jnp.where(inside, tile, jnp.zeros_like(tile))
    pl.semaphore_wait(barrier, len(others))
    scatter_x()
    copies[2].wait()
    prepare_ham()
    prepare_left_ham()
    for s in range(tiles):
        prepare_right_ham(s, row[s, q])
    copies[1].wait()
    prepare_hist(0, tiles)
    zs[0] = sum_x().reshape(zs.shape[1:])
    spread_near()
    scatter_z(0)
    copies[3].wait()
    copies[4].wait()
    near_done()
    prepare_left(near_tile)


    def use_near(g, values):
        for i in range(size):
            s = g * size + i
            early[s] = row[s, q] + F32(STEP) * values[i]

    def use_first(g, values):
        for i in range(size):
            s = g * size + i
            slope[s] = values[i]
            pred[s] = row[s, q] + F32(STEP) * values[i]

    integrate(0)
    gather(0)
    finish(0, use_near)


    for p in range(slots * n_past):
        wanted = start + p - tiles * sec
        inside = (wanted >= 0) & (wanted < tiles)
        tile = early[jnp.clip(wanted, 0, tiles - 1)]
        cx[1, p % slots, p // slots] = jnp.where(inside, tile, jnp.zeros_like(tile))
    scatter_plane()
    zs[1] = sum_plane()
    scatter_z(1)
    window_done(0)
    prepare_left(window_tile(0))
    integrate(1)
    gather(1)
    finish(1, use_first)
    for s in range(tiles):
        prepare_right_ham(s, pred[s])
    window_done(1)
    prepare_left(window_tile(1))
    integrate(2)

    def to_chips(g, values):
        squares = jnp.zeros((rows, LANES), F32)
        for i in range(size):
            s = g * size + i
            after = row[s, q] + F32(0.5 * STEP) * (slope[s] + values[i])
            out[s, y, core] = after
            change = after - pred[s]
            squares = squares + change * change
        norm_p[x * n_past + q] = (norm_p[x * n_past + q] if g else 0) + jnp.sum(squares, axis=0, keepdims=True)

    finish(2, to_chips)

    def shared(buffer, number, n):
        wait_bytes(buffer.at[pl.ds(0, n - 1)], n_sem.at[number, 1])
        total = buffer[0]
        for i in range(1, n):
            total = total + buffer[i]
        return total

    block = norm_p.at[x * n_past + q]
    for d in plane:
        send(block, block, n_sem.at[0, 0], n_sem.at[0, 1], at_plane(d))
    for d in far_first(n_y):
        for g in range(groups):
            block = out.at[pl.ds(g * size, size), y, core]
            send(block, block, oy_send.at[g], oy_recv.at[g], at_past(2 * ((y + d) % n_y) + core))
    norm_z[z] = shared(norm_p, 0, n_x * n_past)
    block = norm_z.at[z]
    for d in far_first(n_z):
        send(block, block, n_sem.at[1, 0], n_sem.at[1, 1], at_z((z + d) % n_z))
    for g in range(groups):
        wait_bytes(rc.at[0, g, pl.ds(0, n_y - 1)], oy_recv.at[g])
        block = out.at[pl.ds(g * size, size), :, core]
        send(block, block, oc_send.at[g], oc_recv.at[g], partner)
    results = []
    for g in range(groups):
        wait_bytes(rc.at[0, g], oc_recv.at[g])
        block = pl.ds(g * size, size)
        results.append(pltpu.make_async_copy(out.at[block], out_hbm.at[block], out_sem.at[g]))
        results[-1].start()
    total = shared(norm_z, 1, n_z)
    mean = jnp.sum(total, axis=1, keepdims=True) * F32(1.0 / entries)
    norm_ref[0] = (jnp.sqrt(jnp.broadcast_to(mean, (1, LANES))) * F32(1.0 / STEP))[0, 0]
    for result in results:
        result.wait()

    wait_bytes(rx, x_sem.at[0])
    wait_bytes(near.at[pl.ds(0, 3 * n_x - 1)], near_sem.at[0])
    wait_bytes(rp.at[pl.ds(0, n_x * n_past - 1)], a_sem.at[0])
    for k in range(2):
        wait_bytes(rz.at[k], z_sem.at[k, 0])
        wait_bytes(win.at[k, pl.ds(0, slots * chunks - 1)], g_sem.at[k, 0])
    for k in range(3):
        for g in range(groups):
            wait_bytes(rc.at[k, g], c_send.at[k, g])
            wait_bytes(ry.at[k, g], y_send.at[k, g])
    for g in range(groups):
        wait_bytes(rc.at[0, g, pl.ds(0, n_y - 1)], oy_send.at[g])
        wait_bytes(rc.at[0, g], oc_send.at[g])
    wait_bytes(norm_p.at[pl.ds(0, n_x * n_past - 1)], n_sem.at[0, 0])
    wait_bytes(norm_z.at[pl.ds(0, n_z - 1)], n_sem.at[1, 0])


def local(n_past, n_second, green_row, green_hist, hamiltonian, quad_table, weight_index, block_start):
    tiles, orbits, _ = green_row.shape
    slots = green_hist.shape[0]
    n_x = CHIPS_X
    n_z = n_second // n_x
    n_y = n_past // 2
    rows = orbits // n_past
    chunks = n_past
    groups = GROUPS if tiles > 4 else 2
    size = tiles // groups
    depth = 2 * slots * orbits
    dims = (
        n_past, n_x, n_z, chunks, slots, tiles, groups,
        1.0 / math.sqrt(orbits * slots * n_past), tiles * n_second * orbits * 2 * orbits,
    )
    dma = pltpu.SemaphoreType.DMA
    scratch = [
        pltpu.SMEM((slots,), jnp.int32),
        pltpu.SMEM(quad_table.shape, F32),
        pltpu.VMEM((tiles, n_past, rows, LANES), F32),
        pltpu.VMEM((slots, tiles, orbits, LANES), F32),
        pltpu.VMEM((orbits, LANES), F32),
        pltpu.VMEM((3 * n_x, chunks, rows, LANES), F32),
        pltpu.VMEM((tiles, rows, LANES), F32),
        pltpu.VMEM((depth, tiles * LANES), BF16),
        pltpu.VMEM((depth, tiles * LANES), BF16),
        pltpu.VMEM((LANES, tiles * LANES), BF16),
        pltpu.VMEM((2 * LANES, depth), BF16),
        pltpu.VMEM((LANES, LANES), BF16),
        pltpu.VMEM((2, n_x, n_past, rows, LANES), F32),
        pltpu.VMEM((n_x - 1, n_past, rows, LANES), F32),
        pltpu.VMEM((n_x * n_past, rows, LANES), F32),
        pltpu.VMEM((2, chunks, rows, LANES), F32),
        pltpu.VMEM((2, n_z - 1, rows, LANES), F32),
        pltpu.VMEM((2, slots * chunks, rows, LANES), F32),
        pltpu.VMEM((3, groups, 2, n_y, size, rows, LANES), F32),
        pltpu.VMEM((3, groups, n_y, size, rows, LANES), F32),
        pltpu.VMEM((3, groups, n_y, size, rows, LANES), F32),
        pltpu.VMEM((3, groups, n_y - 1, size, rows, LANES), F32),
        pltpu.VMEM((max(tiles, n_past), rows, LANES), F32),
        pltpu.VMEM((tiles, rows, LANES), F32),
        pltpu.VMEM((n_x * n_past, 1, LANES), F32),
        pltpu.VMEM((n_z, 1, LANES), F32),
        pltpu.VMEM((tiles, n_y, 2, rows, LANES), F32),
        dma((5,)),
        dma((2,)),
        dma((2,)),
        dma((2,)),
        dma((2, 2)),
        dma((2, 2)),
        dma((3, groups)), dma((3, groups)),
        dma((3, groups)), dma((3, groups)),
        dma((groups,)), dma((groups,)),
        dma((groups,)), dma((groups,)),
        dma((2, 2)),
        dma((groups,)),
    ]
    smem = pl.BlockSpec(memory_space=pltpu.SMEM)
    anywhere = pl.BlockSpec(memory_space=pl.ANY)
    after, change = pl.pallas_call(
        functools.partial(kernel, dims),
        out_shape=(
            jax.ShapeDtypeStruct((tiles, n_y, 2, rows, LANES), F32),
            jax.ShapeDtypeStruct((1,), F32),
        ),
        in_specs=[smem] + [anywhere] * 5,
        out_specs=(anywhere, smem),
        scratch_shapes=scratch,
        compiler_params=pltpu.CompilerParams(
            collective_id=0, has_side_effects=True, vmem_limit_bytes=60 * 1024 * 1024
        ),
    )(
        block_start, weight_index, quad_table,
        green_row.reshape(tiles, n_past, rows, LANES), green_hist, hamiltonian,
    )
    return after.reshape(tiles, orbits, LANES), change


def solution(mesh):
    placed = (P("second", None, None), P("past", "second", None, None), P(), P(), P("past"), P())
    return jax.shard_map(
        functools.partial(local, mesh.shape["past"], mesh.shape["second"]),
        mesh=mesh,
        in_specs=placed,
        out_specs=(P("second", None, None), P()),
        check_vma=False,
    )
```

```python
import functools
import math

import jax
import jax.numpy as jnp
from jax import lax
from jax.experimental import pallas as pl
from jax.experimental.pallas import tpu as pltpu
from jax.sharding import PartitionSpec as P

COUPLING = 0.5
STEP = 0.25
PRODUCTS = 1
GROUPS = 4
CHIPS_X = 4
LANES = 128
MESH = pl.DeviceIdType.MESH
F32 = jnp.float32
BF16 = jnp.bfloat16


def wait_bytes(ref, sem):
    pltpu.make_async_copy(ref, ref, sem).wait()


def send(src, dst, send_sem, recv_sem, where):
    pltpu.make_async_remote_copy(
        src_ref=src, dst_ref=dst, send_sem=send_sem, recv_sem=recv_sem, device_id=where, device_id_type=MESH
    ).start()


def far_first(n):
    return sorted(range(1, n), key=lambda d: -min(d, n - d))


def split(values):
    high = values.astype(BF16).astype(F32)
    return high, values - high


def kernel(
    dims, start_ref, index_hbm, table_hbm, row_hbm, hist_hbm, ham_hbm, out_hbm, norm_ref,
    index_ref, table_ref, row, hist, ham_ref, near, early, r_high, r_low, r_ham, left, l_ham, cx, rx, rp, zs, rz, win,
    part, rc, sc, ry, slope, pred, norm_p, norm_z, out,
    in_sem, x_sem, near_sem, a_sem, z_sem, g_sem, c_send, c_recv, y_send, y_recv,
    oy_send, oy_recv, oc_send, oc_recv, n_sem, out_sem,
):
    n_past, n_x, n_z, chunks, slots, tiles, groups, norm_scale, entries = dims
    n_y = n_past // 2
    size = tiles // groups
    half = LANES // 2
    q, sec = lax.axis_index("past"), lax.axis_index("second")
    z, x = sec // n_x, sec % n_x
    y, core = q // 2, q % 2
    mine = z % chunks
    rows = row.shape[2]

    def at_x(x_to):
        return (q, z * n_x + x_to)

    def at_z(z_to):
        return (q, z_to * n_x + x)

    def at_past(past_to):
        return (past_to, sec)

    def at_plane(d):
        return (2 * ((y + d[0]) % n_y) + (core + d[1]) % 2, z * n_x + (x + d[2]) % n_x)

    plane = [(a, b, c) for a in range(n_y) for b in range(2) for c in range(n_x)][1:]
    plane.sort(key=lambda d: -min(d[0], n_y - d[0]) - min(d[2], n_x - d[2]))
    partner = at_past(2 * y + (1 - core))

    copies = []
    for source, target in (
        (row_hbm, row), (hist_hbm, hist), (ham_hbm, ham_ref),
        (index_hbm, index_ref), (table_hbm, table_ref),
    ):
        copies.append(pltpu.make_async_copy(source, target, in_sem.at[len(copies)]))

    copies[0].start()
    barrier = pltpu.get_barrier_semaphore()
    reach = min(chunks // 2, n_z // 2)
    others = [at_z((z + d) % n_z) for d in far_first(n_z)]
    others += [
        (q, (z + e) % n_z * n_x + (x + d) % n_x)
        for e in far_first(n_z)
        if min(e, n_z - e) <= reach
        for d in range(1, n_x)
    ]
    others += [at_plane(d) for d in plane]
    for other in others:
        pl.semaphore_signal(barrier, inc=1, device_id=other, device_id_type=MESH)


    lane = lax.broadcasted_iota(jnp.int32, (1, LANES), 1)
    real = lane < half
    turn = jnp.where(real, F32(1), F32(-1))

    def swap(values):
        return pltpu.roll(values, half, axis=values.ndim - 1)

    def self_energy(values):
        square = values * values
        return (square + swap(square)) * values * F32(-COUPLING)


    def scatter_x():
        for d in far_first(n_x):
            to = (x + d) % n_x
            send(cx.at[0, to], rx.at[d - 1], x_sem.at[0], x_sem.at[1], at_x(to))

    def sum_x():
        wait_bytes(rx, x_sem.at[1])
        total = cx[0, x]
        for d in range(n_x - 1):
            total = total + rx[d]
        return total

    def scatter_plane():
        for d in plane:
            to, column = at_plane(d)
            block = cx.at[1, column % n_x, to]
            send(block, rp.at[x * n_past + q], a_sem.at[0], a_sem.at[1], (to, column))
        rp[x * n_past + q] = cx[1, x, q]

    def sum_plane():
        wait_bytes(rp.at[pl.ds(0, n_x * n_past - 1)], a_sem.at[1])
        total = rp[pl.ds(0, n_past)]
        for i in range(1, n_x):
            total = total + rp[pl.ds(i * n_past, n_past)]
        return total


    def spread_near():
        for to in range(n_x):
            beside = (z + 1) % n_z if to < n_x // 2 else (z + n_z - 1) % n_z
            send(zs.at[0], near.at[n_x + x], near_sem.at[0], near_sem.at[1], (q, beside * n_x + to))
        for d in far_first(n_x):
            send(zs.at[0], near.at[x], near_sem.at[0], near_sem.at[1], at_x((x + d) % n_x))
        near[x] = zs[0]

    def near_done():
        wait_bytes(near.at[pl.ds(0, 2 * n_x - 1)], near_sem.at[1])

    def near_tile(t):
        return (near[t] + near[n_x + t]).reshape(half, LANES)

    def scatter_z(k):
        for d in far_first(n_z):
            to = (z + d) % n_z
            send(zs.at[k, to % chunks], rz.at[k, d - 1], z_sem.at[k, 0], z_sem.at[k, 1], at_z(to))

    def gather(k):
        wait_bytes(rz.at[k], z_sem.at[k, 1])
        total = zs[k, mine]
        for d in range(n_z - 1):
            total = total + rz[k, d]
        win[k, x * chunks + mine] = total
        block = win.at[k, x * chunks + mine]
        for e in sorted(range(1 - chunks // 2, chunks // 2 + 1), key=lambda e: -abs(e)):
            for d in far_first(n_x) + [0]:
                if d or e:
                    where = (q, (z + e + n_z) % n_z * n_x + (x + d) % n_x)
                    send(block, block, g_sem.at[k, 0], g_sem.at[k, 1], where)

    def window_done(k):
        wait_bytes(win.at[k, pl.ds(0, slots * chunks - 1)], g_sem.at[k, 1])

    def window_tile(k):
        return lambda t: win[k, pl.ds(t * chunks, chunks)].reshape(half, LANES)


    def prepare_hist(first, last):
        def body(s, carry):
            columns = pl.ds(pl.multiple_of(s * LANES, LANES), LANES)
            for p in range(slots):
                tile = hist[p, s]
                for kind, values in enumerate((tile, self_energy(tile))):
                    high, low = split(values)
                    at = pl.ds((2 * p + kind) * half, half)
                    r_high[at, columns] = high.astype(BF16)
                    r_low[at, columns] = low.astype(BF16)
            return carry

        lax.fori_loop(first, last, body, 0)

    def prepare_ham():
        tile = ham_ref[...]
        flipped = jnp.concatenate([tile, jnp.zeros_like(tile)], axis=0).T
        ham = F32(0.5) * (tile * turn + flipped[:half] + swap(flipped[half:]))
        slope[pl.ds(0, n_past)] = ham.reshape(n_past, rows, LANES)

    def prepare_left_ham():
        high, low = split(slope[q])
        blank = jnp.zeros((LANES - 3 * rows, LANES), F32)
        l_ham[...] = jnp.concatenate([high, high, low, blank], axis=0).T.astype(BF16)
        r_ham[...] = jnp.zeros(r_ham.shape, BF16)

    def prepare_right_ham(s, values):
        high, low = split(values)
        both = jnp.concatenate([high, low, high, jnp.zeros_like(high)], axis=0)
        r_ham[pl.ds(0, 4 * rows), pl.ds(s * LANES, LANES)] = both.astype(BF16)

    def prepare_left(tile_of):
        for t in range(slots):
            weight = table_ref[index_ref[t]] * F32(norm_scale)
            tile = tile_of(t)
            first = weight * self_energy(tile)
            second = weight * tile
            real_part = jnp.where(real, first, swap(second))
            imag_part = jnp.where(real, swap(first), second)
            high, low = split(jnp.concatenate([real_part, imag_part], axis=0))
            left[pl.ds(0, LANES), pl.ds(t * LANES, LANES)] = high.astype(BF16)
            left[pl.ds(LANES, LANES), pl.ds(t * LANES, LANES)] = low.astype(BF16)

    def contract(k, number):
        wide = tiles // PRODUCTS
        columns = pl.ds(number * wide * LANES, wide * LANES)
        both = jnp.dot(left[...], r_high[:, columns], preferred_element_type=F32)
        more = jnp.dot(left[pl.ds(0, LANES), :], r_low[:, columns], preferred_element_type=F32)
        ham = jnp.dot(l_ham[...], r_ham[:, columns], preferred_element_type=F32)
        total = both[:LANES] + both[LANES:] + more + ham
        for i in range(wide):
            at = slice(i * LANES, (i + 1) * LANES)
            tile = total[:half, at] - turn * swap(total[half:, at])
            g, s = divmod(number * wide + i, size)
            for p in range(n_past):
                part[k, g, p % 2, p // 2, s] = tile[p * rows : (p + 1) * rows]
            if s == size - 1:
                send(part.at[k, g, 1 - core], rc.at[k, g], c_send.at[k, g], c_recv.at[k, g], partner)

    def between_chips(k):
        for g in range(groups):
            wait_bytes(rc.at[k, g], c_recv.at[k, g])
            sc[k, g] = part[k, g, core] + rc[k, g]
        for d in far_first(n_y):
            to = (y + d) % n_y
            for g in range(groups):
                send(sc.at[k, g, to], ry.at[k, g, d - 1], y_send.at[k, g], y_recv.at[k, g], at_past(2 * to + core))

    def slope_of(k, g):
        wait_bytes(ry.at[k, g], y_recv.at[k, g])
        total = sc[k, g, y]
        for d in range(n_y - 1):
            total = total + ry[k, g, d]
        return turn * swap(total.reshape(size * rows, LANES)).reshape(size, rows, LANES)

    def integrate(k):
        for number in range(PRODUCTS):
            contract(k, number)
        between_chips(k)

    def finish(k, use):
        for g in range(groups):
            use(g, slope_of(k, g))


    start = start_ref[0]
    copies[0].wait()
    for copy in copies[1:]:
        copy.start()
    for t in range(slots):
        wanted = start + slots * q + t - tiles * sec
        inside = (wanted >= 0) & (wanted < tiles)
        tile = row[jnp.clip(wanted, 0, tiles - 1)]
        cx[0, t] = jnp.where(inside, tile, jnp.zeros_like(tile))
    pl.semaphore_wait(barrier, len(others))
    scatter_x()
    copies[2].wait()
    prepare_ham()
    prepare_left_ham()
    for s in range(tiles):
        prepare_right_ham(s, row[s, q])
    copies[1].wait()
    prepare_hist(0, tiles)
    zs[0] = sum_x().reshape(zs.shape[1:])
    spread_near()
    scatter_z(0)
    copies[3].wait()
    copies[4].wait()
    near_done()
    prepare_left(near_tile)


    def use_near(g, values):
        for i in range(size):
            s = g * size + i
            early[s] = row[s, q] + F32(STEP) * values[i]

    def use_first(g, values):
        for i in range(size):
            s = g * size + i
            slope[s] = values[i]
            pred[s] = row[s, q] + F32(STEP) * values[i]

    integrate(0)
    gather(0)
    finish(0, use_near)


    for p in range(slots * n_past):
        wanted = start + p - tiles * sec
        inside = (wanted >= 0) & (wanted < tiles)
        tile = early[jnp.clip(wanted, 0, tiles - 1)]
        cx[1, p % slots, p // slots] = jnp.where(inside, tile, jnp.zeros_like(tile))
    scatter_plane()
    zs[1] = sum_plane()
    scatter_z(1)
    window_done(0)
    prepare_left(window_tile(0))
    integrate(1)
    gather(1)
    finish(1, use_first)
    for s in range(tiles):
        prepare_right_ham(s, pred[s])
    window_done(1)
    prepare_left(window_tile(1))
    integrate(2)

    def to_chips(g, values):
        squares = jnp.zeros((rows, LANES), F32)
        for i in range(size):
            s = g * size + i
            after = row[s, q] + F32(0.5 * STEP) * (slope[s] + values[i])
            out[s, y, core] = after
            change = after - pred[s]
            squares = squares + change * change
        norm_p[x * n_past + q] = (norm_p[x * n_past + q] if g else 0) + jnp.sum(squares, axis=0, keepdims=True)

    finish(2, to_chips)

    def shared(buffer, number, n):
        wait_bytes(buffer.at[pl.ds(0, n - 1)], n_sem.at[number, 1])
        total = buffer[0]
        for i in range(1, n):
            total = total + buffer[i]
        return total

    block = norm_p.at[x * n_past + q]
    for d in plane:
        send(block, block, n_sem.at[0, 0], n_sem.at[0, 1], at_plane(d))
    for d in far_first(n_y):
        for g in range(groups):
            block = out.at[pl.ds(g * size, size), y, core]
            send(block, block, oy_send.at[g], oy_recv.at[g], at_past(2 * ((y + d) % n_y) + core))
    norm_z[z] = shared(norm_p, 0, n_x * n_past)
    block = norm_z.at[z]
    for d in far_first(n_z):
        send(block, block, n_sem.at[1, 0], n_sem.at[1, 1], at_z((z + d) % n_z))
    for g in range(groups):
        wait_bytes(rc.at[0, g, pl.ds(0, n_y - 1)], oy_recv.at[g])
        block = out.at[pl.ds(g * size, size), :, core]
        send(block, block, oc_send.at[g], oc_recv.at[g], partner)
    results = []
    for g in range(groups):
        wait_bytes(rc.at[0, g], oc_recv.at[g])
        block = pl.ds(g * size, size)
        results.append(pltpu.make_async_copy(out.at[block], out_hbm.at[block], out_sem.at[g]))
        results[-1].start()
    total = shared(norm_z, 1, n_z)
    mean = jnp.sum(total, axis=1, keepdims=True) * F32(1.0 / entries)
    norm_ref[0] = (jnp.sqrt(jnp.broadcast_to(mean, (1, LANES))) * F32(1.0 / STEP))[0, 0]
    for result in results:
        result.wait()

    wait_bytes(rx, x_sem.at[0])
    wait_bytes(near.at[pl.ds(0, 2 * n_x - 1)], near_sem.at[0])
    wait_bytes(rp.at[pl.ds(0, n_x * n_past - 1)], a_sem.at[0])
    for k in range(2):
        wait_bytes(rz.at[k], z_sem.at[k, 0])
        wait_bytes(win.at[k, pl.ds(0, slots * chunks - 1)], g_sem.at[k, 0])
    for k in range(3):
        for g in range(groups):
            wait_bytes(rc.at[k, g], c_send.at[k, g])
            wait_bytes(ry.at[k, g], y_send.at[k, g])
    for g in range(groups):
        wait_bytes(rc.at[0, g, pl.ds(0, n_y - 1)], oy_send.at[g])
        wait_bytes(rc.at[0, g], oc_send.at[g])
    wait_bytes(norm_p.at[pl.ds(0, n_x * n_past - 1)], n_sem.at[0, 0])
    wait_bytes(norm_z.at[pl.ds(0, n_z - 1)], n_sem.at[1, 0])


def local(n_past, n_second, green_row, green_hist, hamiltonian, quad_table, weight_index, block_start):
    tiles, orbits, _ = green_row.shape
    slots = green_hist.shape[0]
    n_x = CHIPS_X
    n_z = n_second // n_x
    n_y = n_past // 2
    rows = orbits // n_past
    chunks = n_past
    groups = GROUPS if tiles > 4 else 2
    size = tiles // groups
    depth = 2 * slots * orbits
    dims = (
        n_past, n_x, n_z, chunks, slots, tiles, groups,
        1.0 / math.sqrt(orbits * slots * n_past), tiles * n_second * orbits * 2 * orbits,
    )
    dma = pltpu.SemaphoreType.DMA
    scratch = [
        pltpu.SMEM((slots,), jnp.int32),
        pltpu.SMEM(quad_table.shape, F32),
        pltpu.VMEM((tiles, n_past, rows, LANES), F32),
        pltpu.VMEM((slots, tiles, orbits, LANES), F32),
        pltpu.VMEM((orbits, LANES), F32),
        pltpu.VMEM((2 * n_x, chunks, rows, LANES), F32),
        pltpu.VMEM((tiles, rows, LANES), F32),
        pltpu.VMEM((depth, tiles * LANES), BF16),
        pltpu.VMEM((depth, tiles * LANES), BF16),
        pltpu.VMEM((LANES, tiles * LANES), BF16),
        pltpu.VMEM((2 * LANES, depth), BF16),
        pltpu.VMEM((LANES, LANES), BF16),
        pltpu.VMEM((2, n_x, n_past, rows, LANES), F32),
        pltpu.VMEM((n_x - 1, n_past, rows, LANES), F32),
        pltpu.VMEM((n_x * n_past, rows, LANES), F32),
        pltpu.VMEM((2, chunks, rows, LANES), F32),
        pltpu.VMEM((2, n_z - 1, rows, LANES), F32),
        pltpu.VMEM((2, slots * chunks, rows, LANES), F32),
        pltpu.VMEM((3, groups, 2, n_y, size, rows, LANES), F32),
        pltpu.VMEM((3, groups, n_y, size, rows, LANES), F32),
        pltpu.VMEM((3, groups, n_y, size, rows, LANES), F32),
        pltpu.VMEM((3, groups, n_y - 1, size, rows, LANES), F32),
        pltpu.VMEM((max(tiles, n_past), rows, LANES), F32),
        pltpu.VMEM((tiles, rows, LANES), F32),
        pltpu.VMEM((n_x * n_past, 1, LANES), F32),
        pltpu.VMEM((n_z, 1, LANES), F32),
        pltpu.VMEM((tiles, n_y, 2, rows, LANES), F32),
        dma((5,)),
        dma((2,)),
        dma((2,)),
        dma((2,)),
        dma((2, 2)),
        dma((2, 2)),
        dma((3, groups)), dma((3, groups)),
        dma((3, groups)), dma((3, groups)),
        dma((groups,)), dma((groups,)),
        dma((groups,)), dma((groups,)),
        dma((2, 2)),
        dma((groups,)),
    ]
    smem = pl.BlockSpec(memory_space=pltpu.SMEM)
    anywhere = pl.BlockSpec(memory_space=pl.ANY)
    after, change = pl.pallas_call(
        functools.partial(kernel, dims),
        out_shape=(
            jax.ShapeDtypeStruct((tiles, n_y, 2, rows, LANES), F32),
            jax.ShapeDtypeStruct((1,), F32),
        ),
        in_specs=[smem] + [anywhere] * 5,
        out_specs=(anywhere, smem),
        scratch_shapes=scratch,
        compiler_params=pltpu.CompilerParams(
            collective_id=0, has_side_effects=True, vmem_limit_bytes=60 * 1024 * 1024
        ),
    )(
        block_start, weight_index, quad_table,
        green_row.reshape(tiles, n_past, rows, LANES), green_hist, hamiltonian,
    )
    return after.reshape(tiles, orbits, LANES), change


def solution(mesh):
    placed = (P("second", None, None), P("past", "second", None, None), P(), P(), P("past"), P())
    return jax.shard_map(
        functools.partial(local, mesh.shape["past"], mesh.shape["second"]),
        mesh=mesh,
        in_specs=placed,
        out_specs=(P("second", None, None), P()),
        check_vma=False,
    )
```
